512 devices in a mesh: dp: 64 (over x, z_lo, y), tensor: 8 (over z_hi, core).
Axes of the slice: x: 4, y: 4, z: 16 (z_hi: 4, z_lo: 4; z = z_hi * 4 + z_lo), core: 2. Of those that a mesh axis runs over, the one named last changes fastest.
Arguments:
- grad_a: bfloat16 [64, 8, 1024, 3, 64], P('dp', 'tensor'), may hold values from -70 to 70
- grad_b: bfloat16 [64, 64, 8, 1280], P('dp', None, 'tensor'), may hold values from -70 to 70
- params_a: float32 [8, 1024, 3, 64], P('tensor', 'dp'), may hold values from -0.0625 to 0.0625
- params_b: float32 [64, 8, 1280], P('dp', 'tensor'), may hold values from -0.75 to 0.75
- moment_a: float32 [8, 1024, 3, 64], P('tensor', 'dp'), may hold values from -0.00012207031 to 0.00012207031
- moment_b: float32 [64, 8, 1280], P('dp', 'tensor'), may hold values from -0.00012207031 to 0.00012207031
- second_a: float32 [8, 1024, 3, 64], P('tensor', 'dp'), may hold values from 1e-08 to 1e-07
- second_b: float32 [64, 8, 1280], P('dp', 'tensor'), may hold values from 1e-08 to 1e-07
- hidden_in: bfloat16 [4, 512, 8192], P(None, 'dp'), may hold values from -6 to 6
- base_q: bfloat16 [4, 512, 8, 1024], P(None, 'dp', 'tensor'), may hold values from -32 to 32
- base_kv: bfloat16 [4, 512, 8, 256], P(None, 'dp', 'tensor'), may hold values from -6 to 6
- cache_keys: bfloat16 [512, 8, 512, 128], P('dp', 'tensor'), may hold values from -17 to 17
- cache_values: bfloat16 [512, 8, 512, 128], P('dp', 'tensor'), may hold values from -6 to 6
- lengths: int32 [512], P('dp'), may hold values from 2 to 512, as said below
Outputs:
- attention: bfloat16 [4, 512, 8, 1024], P(None, 'dp', 'tensor')
- new_a: float32 [8, 1024, 3, 64], P('tensor', 'dp')
- new_b: float32 [64, 8, 1280], P('dp', 'tensor')
The draws below stay inside these ranges and needn't reach their ends.
Inputs may be any that keep to these rules, and one draw needn't show every extreme that they name: `lengths`: the first of each block of 8 rows holds exactly 512.
All inputs are finite; a program needn't handle non-finite values.
Results may differ from the reference program's by a relative error of at most 0.017.
The reference program's roundings to bfloat16 on the way count: a program that leaves them out, or rounds other values in their place, can miss the bound.
Values may be sent and summed in bfloat16 or wider, within the bound.
No kernel may reach another device: no remote copies, remote signals or barrier semaphores. Data moves between devices by JAX's collectives and lax.ppermute only.
A program may use at most 64 MiB of HBM per device.

```python
import math
import jax
import jax.numpy as jnp
from jax import lax

D = 8192
R = 64
KV = 8
QUERY_PER_KV = 8
HEAD_SIZE = 128
W = 1280
ROWS_DEV = 8
CACHE = 512
STEPS = 4
ROWS = 512
N_DP = 64
N_TENSOR = 8


def owner_scale(shard_ids, group_ids, rise):
    place = (shard_ids * N_TENSOR + group_ids).astype(jnp.float32)
    return jnp.sqrt(1.0 + rise * place / (N_DP * N_TENSOR - 1))


def draw_grad_a(key, part):
    key = jax.random.fold_in(key, 21)
    shape = (N_DP, N_TENSOR, D // N_TENSOR, 3, R)
    shard_ids = jnp.arange(D // N_TENSOR) // (D // N_TENSOR // N_DP)
    group_ids = jnp.arange(N_TENSOR)
    replica_ids = jnp.arange(N_DP)
    base = jnp.clip(jax.random.normal(key, shape, jnp.float32), -4.0, 4.0)
    scale = owner_scale(shard_ids[None, :], group_ids[:, None], 9.0)
    paired = jnp.where(replica_ids[:, None] == shard_ids[None, :], 3.0, 1.0)
    full = scale[None, :, :, None, None] * paired[:, None, :, None, None]
    return (base * full).astype(jnp.bfloat16)


def draw_grad_b(key, part):
    key = jax.random.fold_in(key, 22)
    shape = (N_DP, R, KV, W)
    shard_ids = jnp.arange(R) // (R // N_DP)
    group_ids = jnp.arange(KV) // (KV // N_TENSOR)
    replica_ids = jnp.arange(N_DP)
    base = jnp.clip(jax.random.normal(key, shape, jnp.float32), -4.0, 4.0)
    scale = owner_scale(shard_ids[:, None], group_ids[None, :], 9.0)
    paired = jnp.where(replica_ids[:, None] == shard_ids[None, :], 3.0, 1.0)
    full = scale[None, :, :, None] * paired[:, :, None, None]
    return (base * full).astype(jnp.bfloat16)


def draw_base_q(key, part):
    key = jax.random.fold_in(key, 11)
    values = jnp.clip(jax.random.normal(key, (STEPS, ROWS, KV, QUERY_PER_KV * HEAD_SIZE), jnp.float32), -4.0, 4.0)
    return values.astype(jnp.bfloat16)


def draw_cache_keys(key, part):
    key = jax.random.fold_in(key, 12)
    values = jnp.clip(jax.random.normal(key, (ROWS, KV, CACHE, HEAD_SIZE), jnp.float32), -4.0, 4.0)
    return values.astype(jnp.bfloat16)


def draw_lengths(key, part):
    key = jax.random.fold_in(key, 13)
    drawn = jax.random.randint(key, (ROWS,), 2, CACHE + 1, jnp.int32)
    first = jnp.arange(ROWS) % ROWS_DEV == 0
    return jnp.where(first, CACHE, drawn).astype(jnp.int32)


def block_scale(own_key, dims, shards, low, largest):
    level, own = 1.0, jax.random.fold_in(own_key, 6)
    for position, shards_of in shards:
        steps = jnp.exp(jax.random.uniform(jax.random.fold_in(own, position), (shards_of,), jnp.float32, low / len(shards), largest / len(shards)))
        level = level * jnp.repeat(steps, dims[position] // shards_of).reshape([-1 if axis == position else 1 for axis in range(len(dims))])
    return level


def gaussian(key, extent, deviation, limit, split=(), dtype=jnp.bfloat16):
    result = jax.random.normal(key, extent, jnp.float32) * deviation
    if len(split) > 0:
        result = block_scale(key, extent, split, -0.22, 0.18) * result
    return jnp.clip(result, min=-limit, max=limit).astype(dtype)


def setup_inputs(seed: int = 0) -> dict:
    key_list = jax.random.split(jax.random.key(seed), 15)
    grad_a = draw_grad_a(jax.random.fold_in(key_list[14], 71), 0)
    grad_b = draw_grad_b(jax.random.fold_in(key_list[14], 71), 0)
    params_a = gaussian(key_list[2], (N_TENSOR, D // N_TENSOR, 3, R), D ** -0.5, 0.0625, ((0, 8), (1, 64)), jnp.float32)
    params_b = gaussian(key_list[3], (R, KV, W), R ** -0.5, 0.75, ((0, 64), (1, 8)), jnp.float32)
    moment_a = gaussian(key_list[4], (N_TENSOR, D // N_TENSOR, 3, R), 0.00002, 0.00012207031, ((0, 8), (1, 64)), jnp.float32)
    moment_b = gaussian(key_list[5], (R, KV, W), 0.00002, 0.00012207031, ((0, 64), (1, 8)), jnp.float32)
    second_a = jnp.clip(jnp.exp(math.log(1.0000000116860974e-07) - 2.3025851 * jax.random.uniform(key_list[6], (N_TENSOR, D // N_TENSOR, 3, R), jnp.float32) ** block_scale(key_list[6], (N_TENSOR, D // N_TENSOR, 3, R), ((0, 8), (1, 64)), -0.2, 0.2)), 9.99999993922529e-09, 1.0000000116860974e-07)
    second_b = jnp.clip(jnp.exp(math.log(1.0000000116860974e-07) - 2.3025851 * jax.random.uniform(key_list[7], (R, KV, W), jnp.float32) ** block_scale(key_list[7], (R, KV, W), ((0, 64), (1, 8)), -0.2, 0.2)), 9.99999993922529e-09, 1.0000000116860974e-07)
    hidden_in = gaussian(key_list[8], (STEPS, ROWS, D), 1.0, 6.0, ((1, 64),))
    base_q = draw_base_q(jax.random.fold_in(key_list[14], 71), 0)
    base_kv = gaussian(key_list[10], (STEPS, ROWS, KV, 2 * HEAD_SIZE), 1.0, 6.0, ((1, 64), (2, 8)))
    cache_keys = draw_cache_keys(jax.random.fold_in(key_list[14], 71), 0)
    cache_values = gaussian(key_list[12], (ROWS, KV, CACHE, HEAD_SIZE), 1.0, 6.0, ((0, 64), (1, 8)))
    lengths = draw_lengths(jax.random.fold_in(key_list[14], 71), 0)
    return {"grad_a": grad_a, "grad_b": grad_b, "params_a": params_a, "params_b": params_b, "moment_a": moment_a, "moment_b": moment_b, "second_a": second_a, "second_b": second_b, "hidden_in": hidden_in, "base_q": base_q, "base_kv": base_kv, "cache_keys": cache_keys, "cache_values": cache_values, "lengths": lengths}


first_fix = 0.9999734386011124
second_fix = 0.09520785288629038

def adam_update(param, moment, second, grad, clip):
    grad = grad * clip
    moment = 0.9 * moment + 0.1 * grad
    second = 0.999 * second + 0.001 * grad * grad
    first_hat = moment / first_fix
    second_hat = second / second_fix
    return param - 0.1 * first_hat / (jnp.sqrt(second_hat) + 1e-08)

def attend_step(query, key, value, cache_keys, cache_values, lengths, step):
    rows = query.shape[1]
    q_now = query[step].reshape(rows, KV, QUERY_PER_KV, HEAD_SIZE).astype(jnp.float32)
    inv = HEAD_SIZE ** (-0.5)
    cached = jnp.einsum('bhgd,bhpd->bhgp', q_now, cache_keys.astype(jnp.float32)) * inv
    live = jnp.arange(CACHE)[None, :] < lengths[:, None]
    cached = jnp.where(live[:, None, None, :], cached, -jnp.inf)
    fresh = jnp.einsum('bhgd,sbhd->bhgs', q_now, key[:step + 1].astype(jnp.float32)) * inv
    top = jnp.maximum(lax.optimization_barrier(jnp.max(cached, axis=-1)), lax.optimization_barrier(jnp.max(fresh, axis=-1)))
    e_cached = jnp.exp(cached - top[..., None])
    e_fresh = jnp.exp(fresh - top[..., None])
    total = lax.optimization_barrier(jnp.sum(e_cached, axis=-1)) + lax.optimization_barrier(jnp.sum(e_fresh, axis=-1))
    w_cached = e_cached.astype(jnp.bfloat16).astype(jnp.float32)
    w_fresh = e_fresh.astype(jnp.bfloat16).astype(jnp.float32)
    out = jnp.einsum('bhgp,bhpd->bhgd', w_cached, cache_values.astype(jnp.float32))
    out = out + jnp.einsum('bhgs,sbhd->bhgd', w_fresh, value[:step + 1].astype(jnp.float32))
    out = out / total[..., None]
    return out.astype(jnp.bfloat16).reshape(rows, KV, QUERY_PER_KV * HEAD_SIZE)

def reference(grad_a, grad_b, params_a, params_b, moment_a, moment_b, second_a, second_b, hidden_in, base_q, base_kv, cache_keys, cache_values, lengths):
    mean_a = lax.optimization_barrier(jnp.sum(grad_a.astype(jnp.float32), axis=0)) / N_DP
    mean_b = lax.optimization_barrier(jnp.sum(grad_b.astype(jnp.float32), axis=0)) / N_DP
    norm = jnp.sqrt(jnp.sum(mean_a * mean_a) + jnp.sum(mean_b * mean_b))
    clip = jnp.minimum(1.0, 1.0 / (norm + 1e-06))
    new_a = adam_update(params_a, moment_a, second_a, mean_a, clip)
    new_b = adam_update(params_b, moment_b, second_b, mean_b, clip)
    adapter_a = new_a.astype(jnp.bfloat16).reshape(D, 3 * R)
    adapter_b = new_b.astype(jnp.bfloat16)
    rows = hidden_in.shape[1]
    flat = hidden_in.reshape(STEPS * rows, D)
    clip_factor = jnp.dot(flat, adapter_a, preferred_element_type=jnp.float32).astype(jnp.bfloat16)
    clip_factor = clip_factor.reshape(STEPS, rows, 3, R).astype(jnp.float32)
    adapter_b_float = adapter_b.astype(jnp.float32)
    query_delta = jnp.einsum('alo,oei->alei', clip_factor[:, :, 0], adapter_b_float[:, :, :QUERY_PER_KV * HEAD_SIZE])
    key_delta = jnp.einsum('alo,oei->alei', clip_factor[:, :, 1], adapter_b_float[:, :, QUERY_PER_KV * HEAD_SIZE:(QUERY_PER_KV + 1) * HEAD_SIZE])
    value_delta = jnp.einsum('alo,oei->alei', clip_factor[:, :, 2], adapter_b_float[:, :, (QUERY_PER_KV + 1) * HEAD_SIZE:])
    query = (base_q.astype(jnp.float32) + 2.0 * query_delta).astype(jnp.bfloat16)
    key = (base_kv[..., :HEAD_SIZE].astype(jnp.float32) + 2.0 * key_delta).astype(jnp.bfloat16)
    value = (base_kv[..., HEAD_SIZE:].astype(jnp.float32) + 2.0 * value_delta).astype(jnp.bfloat16)
    outs = [attend_step(query, key, value, cache_keys, cache_values, lengths, step) for step in range(STEPS)]
    return (jnp.stack(outs), new_a, new_b)
```

```python
import jax
import jax.numpy as jnp
from jax import lax
from jax.sharding import PartitionSpec as P

D = 8192
R = 64
QUERY_PER_KV = 8
HEAD_SIZE = 128


first_fix = 0.9999734386011124
second_fix = 0.09520785288629038


def adam_update(param, moment, second, grad, clip):
    grad = grad * clip
    moment = 0.9 * moment + 0.1 * grad
    second = 0.999 * second + 0.001 * grad * grad
    first_hat = moment / first_fix
    second_hat = second / second_fix
    return param - 0.1 * first_hat / (jnp.sqrt(second_hat) + 1e-08)


def attend_step(query, key, value, cache_keys, cache_values, lengths, step):
    rows = query.shape[1]
    heads = query.shape[2]
    slots = cache_keys.shape[2]
    q_now = query[step].reshape(rows, heads, QUERY_PER_KV, HEAD_SIZE)
    inv = HEAD_SIZE ** (-0.5)
    cached = (
        jnp.einsum("bhgd,bhpd->bhgp", q_now, cache_keys, preferred_element_type=jnp.float32) * inv
    )
    live = jnp.arange(slots)[None, :] < lengths[:, None]
    cached = jnp.where(live[:, None, None, :], cached, -jnp.inf)
    fresh = (
        jnp.einsum("bhgd,sbhd->bhgs", q_now, key[: step + 1], preferred_element_type=jnp.float32)
        * inv
    )
    top = jnp.maximum(jnp.max(cached, axis=-1), jnp.max(fresh, axis=-1))
    e_cached = jnp.exp(cached - top[..., None])
    e_fresh = jnp.exp(fresh - top[..., None])
    total = jnp.sum(e_cached, axis=-1) + jnp.sum(e_fresh, axis=-1)
    out = jnp.einsum(
        "bhgp,bhpd->bhgd",
        e_cached.astype(jnp.bfloat16),
        cache_values,
        preferred_element_type=jnp.float32,
    )
    out = out + jnp.einsum(
        "bhgs,sbhd->bhgd",
        e_fresh.astype(jnp.bfloat16),
        value[: step + 1],
        preferred_element_type=jnp.float32,
    )
    out = out / total[..., None]
    return out.astype(jnp.bfloat16).reshape(rows, heads, QUERY_PER_KV * HEAD_SIZE)


def shards(
    grad_a,
    grad_b,
    params_a,
    params_b,
    moment_a,
    moment_b,
    second_a,
    second_b,
    hidden_in,
    base_q,
    base_kv,
    cache_keys,
    cache_values,
    lengths,
):
    replicas = lax.axis_size("dp")
    devices = replicas * lax.axis_size("tensor")
    local_a = params_a.size
    rows_a = grad_a.reshape(replicas, local_a)
    rows_b = grad_b.reshape(replicas, params_b.size)
    sent = jnp.concatenate([rows_a, rows_b], axis=1)
    arrived = lax.all_to_all(sent, "dp", 0, 0, tiled=True)
    mean = jnp.sum(arrived.astype(jnp.float32), axis=0) / replicas
    squares = jnp.broadcast_to(jnp.sum(mean * mean), (devices, 1, 128))
    squares = lax.all_to_all(squares, ("dp", "tensor"), 0, 0, tiled=True)
    squares = jnp.sum(squares[:, 0, 0])
    clip = jnp.minimum(1.0, 1.0 / (jnp.sqrt(squares) + 1e-06))
    new_a = adam_update(params_a, moment_a, second_a, mean[:local_a].reshape(params_a.shape), clip)
    new_b = adam_update(params_b, moment_b, second_b, mean[local_a:].reshape(params_b.shape), clip)
    shard = jnp.concatenate([new_a.reshape(-1), new_b.reshape(-1)]).astype(jnp.bfloat16)
    adapters = lax.all_to_all(
        jnp.broadcast_to(shard, (replicas, shard.size)), "dp", 0, 0, tiled=True
    )
    adapter_a = adapters[:, :local_a].reshape(-1, 3 * R)
    adapter_b = adapters[:, local_a:].reshape(replicas, 1, -1)
    steps, rows = (hidden_in.shape[0], hidden_in.shape[1])
    width = adapter_a.shape[0]
    mine = lax.dynamic_slice_in_dim(hidden_in, lax.axis_index("tensor") * width, width, axis=2)
    partial = jnp.dot(
        mine.reshape(steps * rows, width), adapter_a, preferred_element_type=jnp.float32
    )
    groups = lax.axis_size("tensor")
    partial = lax.all_to_all(
        jnp.broadcast_to(partial.reshape(-1, 128), (groups, partial.size // 128, 128)),
        "tensor", 0, 0, tiled=True,
    )
    shrink = jnp.sum(partial, axis=0).astype(jnp.bfloat16)
    clip_factor = shrink.reshape(steps, rows, 3, R)
    query_delta = jnp.einsum(
        "alo,oei->alei",
        clip_factor[:, :, 0],
        adapter_b[:, :, : QUERY_PER_KV * HEAD_SIZE],
        preferred_element_type=jnp.float32,
    )
    key_delta = jnp.einsum(
        "alo,oei->alei",
        clip_factor[:, :, 1],
        adapter_b[:, :, QUERY_PER_KV * HEAD_SIZE : (QUERY_PER_KV + 1) * HEAD_SIZE],
        preferred_element_type=jnp.float32,
    )
    value_delta = jnp.einsum(
        "alo,oei->alei",
        clip_factor[:, :, 2],
        adapter_b[:, :, (QUERY_PER_KV + 1) * HEAD_SIZE :],
        preferred_element_type=jnp.float32,
    )
    query = (base_q.astype(jnp.float32) + 2.0 * query_delta).astype(jnp.bfloat16)
    key = (base_kv[..., :HEAD_SIZE].astype(jnp.float32) + 2.0 * key_delta).astype(jnp.bfloat16)
    value = (base_kv[..., HEAD_SIZE:].astype(jnp.float32) + 2.0 * value_delta).astype(jnp.bfloat16)
    outputs = [
        attend_step(query, key, value, cache_keys, cache_values, lengths, step)
        for step in range(steps)
    ]
    return (jnp.stack(outputs), new_a, new_b)


def solution(mesh):
    in_specs = (
        P("dp", "tensor", None, None, None),
        P("dp", None, "tensor", None),
        P("tensor", "dp", None, None),
        P("dp", "tensor", None),
        P("tensor", "dp", None, None),
        P("dp", "tensor", None),
        P("tensor", "dp", None, None),
        P("dp", "tensor", None),
        P(None, "dp", None),
        P(None, "dp", "tensor", None),
        P(None, "dp", "tensor", None),
        P("dp", "tensor", None, None),
        P("dp", "tensor", None, None),
        P("dp"),
    )
    out_specs = (
        P(None, "dp", "tensor", None),
        P("tensor", "dp", None, None),
        P("dp", "tensor", None),
    )
    return jax.shard_map(shards, mesh=mesh, in_specs=in_specs, out_specs=out_specs, check_vma=False)
```

```python
import jax
import jax.numpy as jnp
import numpy as np
from jax import lax
from jax.experimental import pallas as pl
from jax.experimental.pallas import tpu as pltpu
from jax.sharding import Mesh
from jax.sharding import PartitionSpec as P

D = 8192
R = 64
QUERY_PER_KV = 8
HEAD_SIZE = 128
STEPS = 4
ROWS = 8
CACHE = 512
TOKENS = STEPS * ROWS
REPLICAS = 64
GROUPS = 8

first_fix = 0.9999734386011124
second_fix = 0.09520785288629038

DP = ("x", "zl", "y")
TENSOR = ("zh", "c")
PLANE = ("x", "y")
NX, NZ, NY = 4, 4, 4
NP = NX * NY

A1, A2, B0 = 0, 64, 96
BLOCK = 136
PADDED = 144
BROWS = PADDED - B0
CHUNKS = 10
OWN1, OWN2, OWN3 = 136, 184, 208
ROW = 240


def shard_id(x, y, z):
    return (x * NZ + z) * NY + y


def tables():
    spread = np.zeros((NP * BROWS, CHUNKS * R), np.float32)
    rank = np.zeros((R, NP * BROWS), np.float32)
    chunk = np.full((1, NP * BROWS), -1, np.int32)
    for x in range(NX):
        for y in range(NY):
            for z in range(NZ):
                d = shard_id(x, y, z)
                for c in range(CHUNKS):
                    row = (x * NY + y) * BROWS + z * CHUNKS + c
                    spread[row, c * R + d] = 1.0
                    rank[d, row] = 1.0
                    chunk[0, row] = c
    order = np.zeros((QUERY_PER_KV * TOKENS,) * 2, np.float32)
    for b in range(ROWS):
        for g in range(QUERY_PER_KV):
            for t in range(STEPS):
                row = (b * QUERY_PER_KV + g) * STEPS + t
                order[row, (g * STEPS + t) * ROWS + b] = 1.0
    return spread, rank, chunk, order


def call(kernel, out_shape, *args, smem=()):
    vmem = pl.BlockSpec(memory_space=pltpu.VMEM)
    scalar = pl.BlockSpec(memory_space=pltpu.SMEM)
    many = isinstance(out_shape, (tuple, list))
    return pl.pallas_call(
        kernel,
        out_shape=out_shape,
        in_specs=[scalar if i in smem else vmem for i in range(len(args))],
        out_specs=[vmem] * len(out_shape) if many else vmem,
        compiler_params=pltpu.CompilerParams(vmem_limit_bytes=48 * 1024 * 1024),
    )(*args)


def dot(a, b):
    return jnp.dot(a, b, preferred_element_type=jnp.float32)


def dot_nt(a, b):
    return lax.dot_general(a, b, (((1,), (1,)), ((), ())), preferred_element_type=jnp.float32)


def pack_kernel(ga_ref, gb_ref, spread_ref, out_ref):
    wide = ga_ref[0:128].T
    narrow = ga_ref[128:192].astype(jnp.float32).T.reshape(REPLICAS, 2, 8, R)
    narrow = jnp.concatenate([narrow[:, 0], narrow[:, 1]], axis=-1)
    gb = gb_ref[...]
    stacked = jnp.concatenate([gb[:, c * 128 : (c + 1) * 128] for c in range(CHUNKS)], axis=0)
    placed = dot(spread_ref[...], stacked).astype(jnp.bfloat16)
    for x in range(NX):
        for y in range(NY):
            at = x * NY + y
            ids = [shard_id(x, y, z) for z in range(NZ)]
            out_ref[at, A1:A2] = jnp.concatenate([wide[16 * d : 16 * d + 16] for d in ids], axis=0)
            out_ref[at, A2:B0] = jnp.concatenate([narrow[d] for d in ids], axis=0).astype(
                jnp.bfloat16
            )
            out_ref[at, B0:PADDED] = placed[at * BROWS : (at + 1) * BROWS]


def partial_kernel(in_ref, pa, pb, ma, mb, sa, sb, out_ref):
    total = in_ref[0].astype(jnp.float32)
    for i in range(1, NP):
        total = total + in_ref[i].astype(jnp.float32)
    pieces = [total[:BLOCK]]
    for ref in (pa, ma, sa):
        pieces.append(jnp.concatenate([ref[0], ref[1]], axis=-1))
    for ref in (pa, ma, sa):
        pieces.append(jnp.concatenate([ref[2, 0:8], ref[2, 8:16]], axis=-1))
    for ref in (pb, mb, sb):
        pieces.append(ref[...])
    pieces.append(jnp.zeros((ROW - OWN3 - 3 * CHUNKS, 128), jnp.float32))
    row = jnp.concatenate(pieces, axis=0)
    for z in range(NZ):
        out_ref[z] = row


def block_mean(in_ref):
    total = in_ref[0, 0:BLOCK]
    for z in range(1, NZ):
        total = total + in_ref[z, 0:BLOCK]
    return total / REPLICAS


def squares_kernel(in_ref, out_ref):
    mean = block_mean(in_ref)
    squares = jnp.sum(mean * mean, axis=0, keepdims=True)
    out_ref[...] = jnp.broadcast_to(squares, out_ref.shape)


def update_kernel(place_ref, squares_ref, in_ref, out_ref, new_a_ref, new_b_ref):
    squares = jnp.sum(squares_ref[...], axis=0, keepdims=True)
    squares = jnp.sum(squares, axis=1, keepdims=True)
    clip = jnp.minimum(1.0, 1.0 / (jnp.sqrt(squares) + 1e-06))
    own = []
    for i in range(3):
        first, second, third = (OWN1 + 16 * i, OWN2 + 8 * i, OWN3 + CHUNKS * i)
        own.append(
            jnp.concatenate(
                [in_ref[z, first : first + 16] for z in range(NZ)]
                + [in_ref[z, second : second + 8] for z in range(NZ)]
                + [in_ref[z, third : third + CHUNKS] for z in range(NZ)],
                axis=0,
            )
        )
    param, moment, second = own
    grad = block_mean(in_ref) * clip
    moment = 0.9 * moment + 0.1 * grad
    second = 0.999 * second + 0.001 * grad * grad
    first_hat = moment / first_fix
    second_hat = second / second_fix
    new = param - 0.1 * first_hat / (jnp.sqrt(second_hat) + 1e-08)
    padded = jnp.concatenate([new, jnp.zeros((PADDED - BLOCK, 128), jnp.float32)], axis=0)
    adapter = padded.astype(jnp.bfloat16)
    for i in range(NP):
        out_ref[i] = adapter
    place = place_ref[0]
    for z in range(NZ):

        @pl.when(place == z)
        def _():
            wide = new[A1 + 16 * z : A1 + 16 * z + 16]
            narrow = new[A2 + 8 * z : A2 + 8 * z + 8]
            new_a_ref[0] = wide[:, :R]
            new_a_ref[1] = wide[:, R:]
            new_a_ref[2, 0:8] = narrow[:, :R]
            new_a_ref[2, 8:16] = narrow[:, R:]
            new_b_ref[...] = new[B0 + CHUNKS * z : B0 + CHUNKS * z + CHUNKS]


def shrink_kernel(group_ref, hidden_ref, in_ref, out_ref):
    del group_ref
    hidden = hidden_ref[...].reshape(TOKENS, D // GROUPS)
    wide, narrow = [], []
    for x in range(NX):
        for z in range(NZ):
            for y in range(NY):
                at = x * NY + y
                wide.append(in_ref[at, A1 + 16 * z : A1 + 16 * z + 16])
    tail = in_ref[:, A2:B0].astype(jnp.float32)
    for x in range(NX):
        for z in range(NZ):
            for y in range(NY):
                piece = tail[x * NY + y, 8 * z : 8 * z + 8]
                narrow += [piece, piece]
    wide = jnp.concatenate(wide, axis=0)
    narrow = jnp.concatenate(narrow, axis=0).astype(jnp.bfloat16)
    lane = lax.broadcasted_iota(jnp.int32, hidden.shape, 1) % 16
    zero = jnp.zeros_like(hidden)
    low = dot(jnp.where(lane < 8, hidden, zero), narrow)
    high = dot(jnp.where(lane < 8, zero, hidden), narrow)
    value = low[:, :R] + high[:, R:]
    value = jnp.concatenate([value[: TOKENS // 2], value[TOKENS // 2 :]], axis=-1)
    partial = jnp.concatenate([dot(hidden, wide), value], axis=0)
    for i in range(GROUPS):
        out_ref[i] = partial


def attend_kernel(
    lengths, parts, adapters, rank, chunk, order, back, base_q, base_kv, keys, values, out_ref
):
    shrink = parts[0]
    for i in range(1, GROUPS):
        shrink = shrink + parts[i]
    value = shrink[TOKENS:]
    value = jnp.concatenate([value[:, :R], value[:, R:]], axis=0)
    stacked = jnp.concatenate([shrink[:TOKENS, :R], shrink[:TOKENS, R:], value], axis=0)
    spread = dot(stacked.astype(jnp.bfloat16), rank[...]).astype(jnp.bfloat16)
    which = chunk[...]
    lhs = []
    for c in range(CHUNKS):
        j = max(0, c - QUERY_PER_KV + 1)
        part = spread[j * TOKENS : (j + 1) * TOKENS]
        lhs.append(jnp.where(which == c, part, jnp.zeros_like(part)))
    rhs = jnp.concatenate([adapters[i, B0:PADDED] for i in range(NP)], axis=0)
    delta = 2.0 * dot(jnp.concatenate(lhs, axis=0), rhs)
    query = []
    for g in range(QUERY_PER_KV):
        base = base_q[:, g * HEAD_SIZE : (g + 1) * HEAD_SIZE].astype(jnp.float32)
        query.append((base + delta[g * TOKENS : (g + 1) * TOKENS]).astype(jnp.bfloat16))
    split = QUERY_PER_KV * TOKENS
    base = base_kv[...].astype(jnp.float32)
    key = (base[:, :HEAD_SIZE] + delta[split : split + TOKENS]).astype(jnp.bfloat16)
    new = (base[:, HEAD_SIZE:] + delta[split + TOKENS :]).astype(jnp.bfloat16)
    query = dot(order[...], jnp.concatenate(query, axis=0)).astype(jnp.bfloat16)
    inv = HEAD_SIZE ** (-0.5)
    fresh = dot_nt(query, key) * inv
    at = lax.broadcasted_iota(jnp.int32, fresh.shape, 0)
    to = lax.broadcasted_iota(jnp.int32, fresh.shape, 1)
    seen = (to % ROWS == at // TOKENS) & (to // ROWS <= at % STEPS)
    fresh = jnp.where(seen, fresh, -jnp.inf)
    slot = lax.broadcasted_iota(jnp.int32, (TOKENS, CACHE), 1)
    outputs = []
    for b in range(ROWS):
        q = query[b * TOKENS : (b + 1) * TOKENS]
        cached = dot_nt(q, keys[b]) * inv
        cached = jnp.where(slot < lengths[b], cached, -jnp.inf)
        late = fresh[b * TOKENS : (b + 1) * TOKENS]
        top = jnp.maximum(
            jnp.max(cached, axis=-1, keepdims=True), jnp.max(late, axis=-1, keepdims=True)
        )
        e_cached = jnp.exp(cached - top)
        e_late = jnp.exp(late - top)
        total = jnp.sum(e_cached, axis=-1, keepdims=True) + jnp.sum(e_late, axis=-1, keepdims=True)
        out = dot(e_cached.astype(jnp.bfloat16), values[b]) + dot(e_late.astype(jnp.bfloat16), new)
        outputs.append((out / total).astype(jnp.bfloat16))
    result = dot(back[...], jnp.concatenate(outputs, axis=0)).astype(jnp.bfloat16)
    for g in range(QUERY_PER_KV):
        out_ref[:, g * HEAD_SIZE : (g + 1) * HEAD_SIZE] = result[g * TOKENS : (g + 1) * TOKENS]


def pack(ga, gb, spread):
    shape = jax.ShapeDtypeStruct((NP, PADDED, 128), jnp.bfloat16)
    return call(pack_kernel, shape, ga, gb, spread)


def partial_row(arrived, *own):
    shape = jax.ShapeDtypeStruct((NZ, ROW, 128), jnp.float32)
    return call(partial_kernel, shape, arrived, *own)


def squares_of(sums):
    shape = jax.ShapeDtypeStruct((NP * GROUPS, 128), jnp.float32)
    return call(squares_kernel, shape, sums)


def update(place, squares, sums):
    shapes = (
        jax.ShapeDtypeStruct((NP, PADDED, 128), jnp.bfloat16),
        jax.ShapeDtypeStruct((3, 16, R), jnp.float32),
        jax.ShapeDtypeStruct((CHUNKS, 128), jnp.float32),
    )
    return call(update_kernel, shapes, place, squares, sums, smem=(0,))


def shrink(group, hidden, adapters):
    width = D // GROUPS
    return pl.pallas_call(
        shrink_kernel,
        out_shape=jax.ShapeDtypeStruct((GROUPS, 48, 128), jnp.float32),
        grid_spec=pltpu.PrefetchScalarGridSpec(
            num_scalar_prefetch=1,
            grid=(1,),
            in_specs=[
                pl.BlockSpec((STEPS, ROWS, width), lambda i, g: (0, 0, g[0])),
                pl.BlockSpec((NP, PADDED, 128), lambda i, g: (0, 0, 0)),
            ],
            out_specs=pl.BlockSpec((GROUPS, 48, 128), lambda i, g: (0, 0, 0)),
        ),
        compiler_params=pltpu.CompilerParams(vmem_limit_bytes=48 * 1024 * 1024),
    )(group, hidden, adapters)


def attend(lengths, parts, adapters, rank, chunk, order, back, base_q, base_kv, keys, values):
    shape = jax.ShapeDtypeStruct((TOKENS, QUERY_PER_KV * HEAD_SIZE), jnp.bfloat16)
    return call(
        attend_kernel, shape, lengths, parts, adapters, rank, chunk, order, back,
        base_q, base_kv, keys, values, smem=(0,),
    )


def natural(a):
    return jnp.transpose(a[0], (1, 0, 2))


def shards(
    grad_a,
    grad_b,
    params_a,
    params_b,
    moment_a,
    moment_b,
    second_a,
    second_b,
    hidden_in,
    base_q,
    base_kv,
    cache_keys,
    cache_values,
    lengths,
):
    spread, rank, chunk, order = tables()
    place = lax.axis_index("zl").reshape(1)
    group = lax.axis_index(TENSOR).reshape(1)
    bf16 = jnp.bfloat16
    ga = jnp.transpose(grad_a[0, 0], (1, 2, 0)).reshape(3 * R, D // GROUPS)
    sent = pack(ga, grad_b[0, :, 0], jnp.asarray(spread, bf16))
    arrived = lax.all_to_all(sent, PLANE, 0, 0, tiled=True)
    own = []
    for a, b in ((params_a, params_b), (moment_a, moment_b), (second_a, second_b)):
        own += [natural(a), b.reshape(CHUNKS, 128)]
    sums = lax.all_to_all(partial_row(arrived, *own), "zl", 0, 0, tiled=True)
    squares = squares_of(sums).reshape(NP * GROUPS, 1, 128)
    squares = lax.all_to_all(squares, PLANE + TENSOR, 0, 0, tiled=True)
    adapters, new_a, new_b = update(place, squares.reshape(NP * GROUPS, 128), sums)
    adapters = lax.all_to_all(adapters, PLANE, 0, 0, tiled=True)
    parts = lax.all_to_all(shrink(group, hidden_in, adapters), TENSOR, 0, 0, tiled=True)
    out = attend(
        lengths,
        parts,
        adapters,
        jnp.asarray(rank, bf16),
        jnp.asarray(chunk),
        jnp.asarray(order, bf16),
        jnp.asarray(order.T, bf16),
        base_q.reshape(TOKENS, -1),
        base_kv.reshape(TOKENS, -1),
        cache_keys.reshape(ROWS, CACHE, HEAD_SIZE),
        cache_values.reshape(ROWS, CACHE, HEAD_SIZE),
    )
    new_a = jnp.transpose(new_a, (1, 0, 2))[None]
    return (out.reshape(STEPS, ROWS, 1, -1), new_a, new_b.reshape(params_b.shape))


def solution(mesh):
    fine = Mesh(mesh.devices.reshape(NX, NZ, NY, 4, 2), DP + TENSOR)
    in_specs = (
        P(DP, TENSOR, None, None, None),
        P(DP, None, TENSOR, None),
        P(TENSOR, DP, None, None),
        P(DP, TENSOR, None),
        P(TENSOR, DP, None, None),
        P(DP, TENSOR, None),
        P(TENSOR, DP, None, None),
        P(DP, TENSOR, None),
        P(None, DP, None),
        P(None, DP, TENSOR, None),
        P(None, DP, TENSOR, None),
        P(DP, TENSOR, None, None),
        P(DP, TENSOR, None, None),
        P(DP),
    )
    out_specs = (
        P(None, DP, TENSOR, None),
        P(TENSOR, DP, None, None),
        P(DP, TENSOR, None),
    )
    return jax.shard_map(shards, mesh=fine, in_specs=in_specs, out_specs=out_specs, check_vma=False)
```

```python
import jax
import jax.numpy as jnp
from jax import lax
from jax.experimental import pallas as pl
from jax.experimental.pallas import tpu as pltpu
from jax.sharding import Mesh
from jax.sharding import PartitionSpec as P

D = 8192
R = 64
QUERY_PER_KV = 8
HEAD_SIZE = 128
STEPS = 4
ROWS = 8
CACHE = 512
TOKENS = STEPS * ROWS
REPLICAS = 64
GROUPS = 8

first_fix = 0.9999734386011124
second_fix = 0.09520785288629038

DP = ("x", "zl", "y")
TENSOR = ("zh", "c")
PLANE = ("x", "y")
NX, NZ, NY = 4, 4, 4
NP = NX * NY

A1, A2, B0 = 0, 64, 96
BLOCK = 136
PADDED = 144
BROWS = PADDED - B0
CHUNKS = 10
OWN1, OWN2, OWN3 = 136, 184, 208
ROW = 240


def shard_id(x, y, z):
    return (x * NZ + z) * NY + y


def call(kernel, out_shape, *args, smem=(), scratch=()):
    vmem = pl.BlockSpec(memory_space=pltpu.VMEM)
    scalar = pl.BlockSpec(memory_space=pltpu.SMEM)
    many = isinstance(out_shape, (tuple, list))
    return pl.pallas_call(
        kernel,
        out_shape=out_shape,
        in_specs=[scalar if i in smem else vmem for i in range(len(args))],
        out_specs=[vmem] * len(out_shape) if many else vmem,
        scratch_shapes=scratch,
        compiler_params=pltpu.CompilerParams(vmem_limit_bytes=48 * 1024 * 1024),
    )(*args)


def dot(a, b):
    return jnp.dot(a, b, preferred_element_type=jnp.float32)


def dot_nt(a, b):
    return lax.dot_general(a, b, (((1,), (1,)), ((), ())), preferred_element_type=jnp.float32)


def one_hot(shape, column_of):
    row = lax.broadcasted_iota(jnp.int32, shape, 0)
    column = lax.broadcasted_iota(jnp.int32, shape, 1)
    return (column_of(row) == column).astype(jnp.float32).astype(jnp.bfloat16)


def pack_kernel(ga_ref, gb_ref, out_ref, rows_ref):
    turn = one_hot((REPLICAS, R), lambda i: ((i // (NY * NZ)) * NZ + i % NZ) * NY + i // NZ % NY)
    turned = dot(turn, gb_ref[...])
    for c in range(CHUNKS):
        rows_ref[pl.ds(c, REPLICAS, stride=CHUNKS), :] = turned[:, c * 128 : (c + 1) * 128]
    wide = ga_ref[0:128].T
    narrow = ga_ref[128:192].astype(jnp.float32).T.reshape(REPLICAS, 2, 8, R)
    narrow = jnp.concatenate([narrow[:, 0], narrow[:, 1]], axis=-1)
    count = NZ * CHUNKS
    none = jnp.zeros((PADDED - BLOCK, 128), jnp.float32)
    for x in range(NX):
        for y in range(NY):
            at = x * NY + y
            ids = [shard_id(x, y, z) for z in range(NZ)]
            out_ref[at, A1:A2] = jnp.concatenate([wide[16 * d : 16 * d + 16] for d in ids], axis=0)
            tail = [narrow[d] for d in ids] + [rows_ref[at * count : (at + 1) * count], none]
            out_ref[at, A2:PADDED] = jnp.concatenate(tail, axis=0).astype(jnp.bfloat16)


def partial_kernel(in_ref, pa, pb, ma, mb, sa, sb, out_ref):
    total = in_ref[0].astype(jnp.float32)
    for i in range(1, NP):
        total = total + in_ref[i].astype(jnp.float32)
    pieces = [total[:BLOCK]]
    for ref in (pa, ma, sa):
        pieces.append(jnp.concatenate([ref[0], ref[1]], axis=-1))
    for ref in (pa, ma, sa):
        pieces.append(jnp.concatenate([ref[2, 0:8], ref[2, 8:16]], axis=-1))
    for ref in (pb, mb, sb):
        pieces += [ref[0, :, c * 128 : (c + 1) * 128] for c in range(CHUNKS)]
    pieces.append(jnp.zeros((ROW - OWN3 - 3 * CHUNKS, 128), jnp.float32))
    row = jnp.concatenate(pieces, axis=0)
    for z in range(NZ):
        out_ref[z] = row


def block_mean(in_ref):
    total = in_ref[0, 0:BLOCK]
    for z in range(1, NZ):
        total = total + in_ref[z, 0:BLOCK]
    return total / REPLICAS


def squares_kernel(in_ref, out_ref):
    mean = block_mean(in_ref)
    squares = jnp.sum(mean * mean, axis=0, keepdims=True)
    out_ref[...] = jnp.broadcast_to(squares, out_ref.shape)


def update_kernel(squares_ref, in_ref, out_ref, new_a_ref, new_b_ref):
    squares = jnp.sum(squares_ref[...], axis=0, keepdims=True)
    squares = jnp.sum(squares, axis=1, keepdims=True)
    clip = jnp.minimum(1.0, 1.0 / (jnp.sqrt(squares) + 1e-06))
    own = []
    for i in range(3):
        first, second, third = (OWN1 + 16 * i, OWN2 + 8 * i, OWN3 + CHUNKS * i)
        own.append(
            jnp.concatenate(
                [in_ref[z, first : first + 16] for z in range(NZ)]
                + [in_ref[z, second : second + 8] for z in range(NZ)]
                + [in_ref[z, third : third + CHUNKS] for z in range(NZ)],
                axis=0,
            )
        )
    param, moment, second = own
    grad = block_mean(in_ref) * clip
    moment = 0.9 * moment + 0.1 * grad
    second = 0.999 * second + 0.001 * grad * grad
    first_hat = moment / first_fix
    second_hat = second / second_fix
    new = param - 0.1 * first_hat / (jnp.sqrt(second_hat) + 1e-08)
    padded = jnp.concatenate([new, jnp.zeros((PADDED - BLOCK, 128), jnp.float32)], axis=0)
    adapter = padded.astype(jnp.bfloat16)
    for i in range(NP):
        out_ref[i] = adapter
    place = lax.axis_index("zl")
    for z in range(NZ):

        @pl.when(place == z)
        def _():
            wide = new[A1 + 16 * z : A1 + 16 * z + 16]
            narrow = new[A2 + 8 * z : A2 + 8 * z + 8]
            new_a_ref[0] = wide[:, :R]
            new_a_ref[1] = wide[:, R:]
            new_a_ref[2, 0:8] = narrow[:, :R]
            new_a_ref[2, 8:16] = narrow[:, R:]
            for c in range(CHUNKS):
                row = B0 + CHUNKS * z + c
                new_b_ref[0, :, c * 128 : (c + 1) * 128] = new[row : row + 1]


def shrink_kernel(hidden_ref, in_ref, out_ref):
    width = D // GROUPS
    group = lax.axis_index("zh") * 2 + lax.axis_index("c")
    start = pl.multiple_of(group * width, width)
    hidden = hidden_ref[:, :, pl.ds(start, width)].reshape(TOKENS, width)
    wide, narrow = [], []
    for x in range(NX):
        for z in range(NZ):
            for y in range(NY):
                at = x * NY + y
                wide.append(in_ref[at, A1 + 16 * z : A1 + 16 * z + 16])
    tail = in_ref[:, A2:B0].astype(jnp.float32)
    for x in range(NX):
        for z in range(NZ):
            for y in range(NY):
                piece = tail[x * NY + y, 8 * z : 8 * z + 8]
                narrow += [piece, piece]
    wide = jnp.concatenate(wide, axis=0)
    narrow = jnp.concatenate(narrow, axis=0).astype(jnp.bfloat16)
    lane = lax.broadcasted_iota(jnp.int32, hidden.shape, 1) % 16
    zero = jnp.zeros_like(hidden)
    low = dot(jnp.where(lane < 8, hidden, zero), narrow)
    high = dot(jnp.where(lane < 8, zero, hidden), narrow)
    value = low[:, :R] + high[:, R:]
    value = jnp.concatenate([value[: TOKENS // 2], value[TOKENS // 2 :]], axis=-1)
    partial = jnp.concatenate([dot(hidden, wide), value], axis=0)
    for i in range(GROUPS):
        out_ref[i] = partial


def attend_kernel(
    lengths, parts, adapters, base_q, base_kv, keys, values, out_ref
):
    shrink = parts[0]
    for i in range(1, GROUPS):
        shrink = shrink + parts[i]
    value = shrink[TOKENS:]
    value = jnp.concatenate([value[:, :R], value[:, R:]], axis=0)
    stacked = jnp.concatenate([shrink[:TOKENS, :R], shrink[:TOKENS, R:], value], axis=0)
    shape = (R, NP * BROWS)
    row = lax.broadcasted_iota(jnp.int32, (1, NP * BROWS), 1)
    at, inside = row // BROWS, row % BROWS
    real = inside < NZ * CHUNKS
    owner = jnp.where(real, ((at // NY) * NZ + inside // CHUNKS) * NY + at % NY, -1)
    rank = (lax.broadcasted_iota(jnp.int32, shape, 0) == owner).astype(jnp.float32)
    spread = dot(stacked.astype(jnp.bfloat16), rank.astype(jnp.bfloat16)).astype(jnp.bfloat16)
    which = jnp.where(real, inside % CHUNKS, -1)
    lhs = []
    for c in range(CHUNKS):
        j = max(0, c - QUERY_PER_KV + 1)
        part = spread[j * TOKENS : (j + 1) * TOKENS]
        lhs.append(jnp.where(which == c, part, jnp.zeros_like(part)))
    rhs = jnp.concatenate([adapters[i, B0:PADDED] for i in range(NP)], axis=0)
    delta = 2.0 * dot(jnp.concatenate(lhs, axis=0), rhs)
    query = []
    for g in range(QUERY_PER_KV):
        base = base_q[:, g * HEAD_SIZE : (g + 1) * HEAD_SIZE].astype(jnp.float32)
        query.append((base + delta[g * TOKENS : (g + 1) * TOKENS]).astype(jnp.bfloat16))
    split = QUERY_PER_KV * TOKENS
    base = base_kv[...].astype(jnp.float32)
    key = (base[:, :HEAD_SIZE] + delta[split : split + TOKENS]).astype(jnp.bfloat16)
    new = (base[:, HEAD_SIZE:] + delta[split + TOKENS :]).astype(jnp.bfloat16)
    size = (QUERY_PER_KV * TOKENS,) * 2
    order = one_hot(size, lambda i: (i % TOKENS) * ROWS + i // TOKENS)
    back = one_hot(size, lambda i: (i % ROWS) * TOKENS + i // ROWS)
    query = dot(order, jnp.concatenate(query, axis=0)).astype(jnp.bfloat16)
    inv = HEAD_SIZE ** (-0.5)
    fresh = dot_nt(query, key) * inv
    at = lax.broadcasted_iota(jnp.int32, fresh.shape, 0)
    to = lax.broadcasted_iota(jnp.int32, fresh.shape, 1)
    seen = (to % ROWS == at // TOKENS) & (to // ROWS <= at % STEPS)
    fresh = jnp.where(seen, fresh, -jnp.inf)
    slot = lax.broadcasted_iota(jnp.int32, (TOKENS, CACHE), 1)
    spans = [slice(b * TOKENS, (b + 1) * TOKENS) for b in range(ROWS)]
    cached = []
    for b in range(ROWS):
        part = dot_nt(query[spans[b]], keys[b]) * inv
        cached.append(jnp.where(slot < lengths[b], part, -jnp.inf))
    cached = jnp.concatenate(cached, axis=0)
    top = jnp.maximum(
        jnp.max(cached, axis=-1, keepdims=True), jnp.max(fresh, axis=-1, keepdims=True)
    )
    e_cached = jnp.exp(cached - top)
    e_fresh = jnp.exp(fresh - top)
    total = jnp.sum(e_cached, axis=-1, keepdims=True) + jnp.sum(e_fresh, axis=-1, keepdims=True)
    weights = e_cached.astype(jnp.bfloat16)
    out = jnp.concatenate([dot(weights[spans[b]], values[b]) for b in range(ROWS)], axis=0)
    out = out + dot(e_fresh.astype(jnp.bfloat16), new)
    result = dot(back, (out / total).astype(jnp.bfloat16)).astype(jnp.bfloat16)
    for g in range(QUERY_PER_KV):
        out_ref[:, g * HEAD_SIZE : (g + 1) * HEAD_SIZE] = result[g * TOKENS : (g + 1) * TOKENS]


def pack(ga, gb):
    shape = jax.ShapeDtypeStruct((NP, PADDED, 128), jnp.bfloat16)
    scratch = [pltpu.VMEM((R * CHUNKS, 128), jnp.float32)]
    return call(pack_kernel, shape, ga, gb, scratch=scratch)


def partial_row(arrived, *own):
    shape = jax.ShapeDtypeStruct((NZ, ROW, 128), jnp.float32)
    return call(partial_kernel, shape, arrived, *own)


def squares_of(sums):
    shape = jax.ShapeDtypeStruct((NP * GROUPS, 128), jnp.float32)
    return call(squares_kernel, shape, sums)


def update(squares, sums):
    shapes = (
        jax.ShapeDtypeStruct((NP, PADDED, 128), jnp.bfloat16),
        jax.ShapeDtypeStruct((3, 16, R), jnp.float32),
        jax.ShapeDtypeStruct((1, 1, CHUNKS * 128), jnp.float32),
    )
    return call(update_kernel, shapes, squares, sums)


def shrink(hidden, adapters):
    shape = jax.ShapeDtypeStruct((GROUPS, 48, 128), jnp.float32)
    return call(shrink_kernel, shape, hidden, adapters)


def attend(lengths, parts, adapters, base_q, base_kv, keys, values):
    shape = jax.ShapeDtypeStruct((TOKENS, QUERY_PER_KV * HEAD_SIZE), jnp.bfloat16)
    return call(
        attend_kernel, shape, lengths, parts, adapters, base_q, base_kv, keys, values, smem=(0,)
    )


def natural(a):
    return jnp.transpose(a[0], (1, 0, 2))


def shards(
    grad_a,
    grad_b,
    params_a,
    params_b,
    moment_a,
    moment_b,
    second_a,
    second_b,
    hidden_in,
    base_q,
    base_kv,
    cache_keys,
    cache_values,
    lengths,
):
    ga = jnp.transpose(grad_a[0, 0], (1, 2, 0)).reshape(3 * R, D // GROUPS)
    sent = pack(ga, grad_b[0, :, 0])
    arrived = lax.all_to_all(sent, PLANE, 0, 0, tiled=True)
    own = []
    for a, b in ((params_a, params_b), (moment_a, moment_b), (second_a, second_b)):
        own += [natural(a), b]
    sums = lax.all_to_all(partial_row(arrived, *own), "zl", 0, 0, tiled=True)
    squares = squares_of(sums).reshape(NP * GROUPS, 1, 128)
    squares = lax.all_to_all(squares, PLANE + TENSOR, 0, 0, tiled=True)
    adapters, new_a, new_b = update(squares.reshape(NP * GROUPS, 128), sums)
    adapters = lax.all_to_all(adapters, PLANE, 0, 0, tiled=True)
    parts = lax.all_to_all(shrink(hidden_in, adapters), TENSOR, 0, 0, tiled=True)
    out = attend(
        lengths,
        parts,
        adapters,
        base_q.reshape(TOKENS, -1),
        base_kv.reshape(TOKENS, -1),
        cache_keys.reshape(ROWS, CACHE, HEAD_SIZE),
        cache_values.reshape(ROWS, CACHE, HEAD_SIZE),
    )
    new_a = jnp.transpose(new_a, (1, 0, 2))[None]
    return (out.reshape(STEPS, ROWS, 1, -1), new_a, new_b)


def solution(mesh):
    fine = Mesh(mesh.devices.reshape(NX, NZ, NY, 4, 2), DP + TENSOR)
    in_specs = (
        P(DP, TENSOR, None, None, None),
        P(DP, None, TENSOR, None),
        P(TENSOR, DP, None, None),
        P(DP, TENSOR, None),
        P(TENSOR, DP, None, None),
        P(DP, TENSOR, None),
        P(TENSOR, DP, None, None),
        P(DP, TENSOR, None),
        P(None, DP, None),
        P(None, DP, TENSOR, None),
        P(None, DP, TENSOR, None),
        P(DP, TENSOR, None, None),
        P(DP, TENSOR, None, None),
        P(DP),
    )
    out_specs = (
        P(None, DP, TENSOR, None),
        P(TENSOR, DP, None, None),
        P(DP, TENSOR, None),
    )
    return jax.shard_map(shards, mesh=fine, in_specs=in_specs, out_specs=out_specs, check_vma=False)
```
